32 devices in a mesh: groups: 2 (over x), dp: 8 (over z, y), tensor: 2 (over core).
Axes of the slice: x: 2, y: 2, z: 4, core: 2. Of those that a mesh axis runs over, the one named last changes fastest.
Arguments:
- output_gradient: bfloat16 [2048, 4096], P(('groups', 'dp'), 'tensor'), parts along dimension 0, may hold values from -6 to 6
- gate_preactivation: bfloat16 [2048, 14336], P(('groups', 'tensor'), 'dp'), parts along dimension 0, may hold values from -6 to 6
- up_preactivation: bfloat16 [2048, 14336], P(('groups', 'tensor'), 'dp'), parts along dimension 0, may hold values from -6 to 6
- frozen_down_weight: bfloat16 [14336, 4096], P('dp', 'tensor'), may hold values from -0.046875 to 0.046875
- adapter_input_factor: bfloat16 [16, 14336, 128], P('groups', 'dp'), parts along dimension 0, may hold values from -0.14941406 to 0.14941406
- adapter_output_factor: bfloat16 [16, 128, 4096], P(('groups', 'dp'), None, 'tensor'), parts along dimension 0, may hold values from -0.14941406 to 0.14941406
- tenant_token_count: int32 [16], P('groups'), parts along dimension 0, may hold values from 1 to 512, 1024 in all
- tenant_owner_index: int32 [16], P('groups'), parts along dimension 0, may hold values from 0 to 7, each once
- token_expert_index: int32 [2048, 2], P('groups'), parts along dimension 0, may hold values from 0 to 7, all different within a row
- routing_weight_pair: float32 [2048, 2], P('groups'), parts along dimension 0, may hold values from 0.2 to 1
Outputs:
- d_gate: bfloat16 [2048, 14336], P(('groups', 'tensor'), 'dp'), parts along dimension 0
- d_up: bfloat16 [2048, 14336], P(('groups', 'tensor'), 'dp'), parts along dimension 0
- grad_a: float32 [16, 14336, 128], P(('groups', 'tensor'), 'dp'), parts along dimension 0
- grad_b: float32 [16, 128, 4096], P(('groups', 'dp'), None, 'tensor'), parts along dimension 0
The draws below stay inside these ranges and needn't reach their ends.
There are 2 independent parts, one for each index of `groups`. The reference program is written for one: setup_inputs(seed, part) draws one part's arguments, and reference() takes and returns one part's arrays. A program takes and returns all parts, laid end to end along the dimension named above; an argument that names none is the same for every part. Nothing has to cross between parts.
Inputs may be any that keep to these rules, and one draw needn't show every extreme that they name: `tenant_token_count`: tenant i holds the tokens from the sum of the counts before it onward; the counts sum to 1024 and the largest is exactly 512. `tenant_owner_index`: each owner index owns exactly one tenant. `token_expert_index`: the two experts of a token differ.
All inputs are finite; a program needn't handle non-finite values.
Results may differ from the reference program's by a relative error of at most 0.001.
Values may be sent and summed in bfloat16 or wider, within the bound.
A program may use at most 128 MiB of HBM per device.

```python
import math
import jax
import jax.numpy as jnp
import numpy as np
from jax import lax

MODEL_WIDTH = 4096
HIDDEN_UNITS = 14336
ADAPTER_EXPERTS = 8
EXPERT_RANK = 16
TOKENS = 1024
TENANT_COUNT = 8
MOST = 512


def steps_of(stream_key, extent, split, low, largest):
    factor_of = 1.0
    for dim, blocks in split:
        heights = jax.random.uniform(jax.random.fold_in(jax.random.fold_in(stream_key, 6), dim), (blocks,), jnp.float32, low / len(split), largest / len(split))
        factor_of = factor_of * jnp.repeat(jnp.exp(heights), extent[dim] // blocks).reshape((-1,) + (1,) * (len(extent) - 1 - dim))
    return factor_of


def choose_distinct(key, rows, amount, top, lift):
    order = jax.random.permutation(jax.random.fold_in(key, 1), amount)
    pull = order
    for power in range(3):
        pull = pull * pull // amount
    pull = pull * lift // amount
    chance = jax.random.randint(jax.random.fold_in(key, 2), (rows, amount), 0, 4096) + pull
    holders = jax.random.permutation(jax.random.fold_in(key, 3), rows)[jnp.arange(amount) % rows]
    chance = jnp.where(jnp.arange(rows)[:, None] == holders[None, :], 1 << 14, chance)
    score = chance * amount + jnp.arange(amount)
    return lax.top_k(score.astype(jnp.int32), top)[1].astype(jnp.int32)


def split_up(amount, total, reach, slope):
    weights = [(1 << 20) // math.isqrt(grade ** slope) + 1 for grade in range(2, amount + 1)]
    spare, counts = total - reach - (amount - 1), [1] * (amount - 1)
    while spare > 0:
        free = [i for i in range(amount - 1) if counts[i] < reach]
        mass, remaining = sum([weights[i] for i in free]), spare
        for i in free:
            more = min(reach - counts[i], max(1, remaining * weights[i] // mass), spare)
            counts[i] = counts[i] + more
            spare = spare - more
    return np.array([reach] + counts)


def ragged_sizes(key, number_of, total, limit, lean):
    if number_of == 2:
        one = jax.random.randint(key, (), max(1, total - limit), min(limit, total - 1) + 1)
        return jnp.stack([one, total - one])
    lengths = jnp.asarray(split_up(number_of, total, limit, lean), jnp.int32)
    twos = (number_of - 1) // 2
    donor, taker = lengths[1:1 + 2 * twos:2], lengths[2:2 + 2 * twos:2]
    room = jnp.minimum(donor - 1, limit - taker)
    passed = jax.random.randint(jax.random.fold_in(key, 1), (twos,), 0, 1 << 20) % (room + 1)
    lengths = lengths.at[1:1 + 2 * twos:2].set(donor - passed).at[2:2 + 2 * twos:2].set(taker + passed)
    return lengths[jax.random.permutation(jax.random.fold_in(key, 2), number_of)]


def normal_values(own_key, extent, scale, bound, shards=(), kind=jnp.bfloat16):
    values = scale * jax.random.normal(own_key, extent, jnp.float32)
    if shards:
        values = values * steps_of(own_key, extent, shards, -0.22, 0.18)
    return jnp.clip(values, -bound, bound).astype(kind)


def setup_inputs(seed: int = 0, part: int = 0) -> dict:
    splits = jax.random.split(jax.random.key(seed), 11)
    own_keys = jax.random.split(jax.random.fold_in(splits[10], part), 11)
    output_gradient = normal_values(own_keys[0], (TOKENS, MODEL_WIDTH), 1.0, 6.0, ((0, 8), (1, 2)))
    gate_preactivation = normal_values(own_keys[1], (TOKENS, HIDDEN_UNITS), 1.0, 6.0, ((0, 2), (1, 8)))
    up_preactivation = normal_values(own_keys[2], (TOKENS, HIDDEN_UNITS), 1.0, 6.0, ((0, 2), (1, 8)))
    frozen_down_weight = normal_values(splits[3], (HIDDEN_UNITS, MODEL_WIDTH), HIDDEN_UNITS ** -0.5, 0.046875, ((0, 8), (1, 2)))
    adapter_input_factor = normal_values(own_keys[4], (TENANT_COUNT, HIDDEN_UNITS, ADAPTER_EXPERTS * EXPERT_RANK), 0.025, 0.14941406, ((1, 8),))
    adapter_output_factor = normal_values(own_keys[5], (TENANT_COUNT, ADAPTER_EXPERTS * EXPERT_RANK, MODEL_WIDTH), 0.025, 0.14941406, ((0, 8), (2, 2)))
    tenant_token_count = ragged_sizes(own_keys[6], TENANT_COUNT, TOKENS, MOST, 2).astype(jnp.int32)
    tenant_owner_index = jax.random.permutation(own_keys[7], TENANT_COUNT).astype(jnp.int32)
    token_expert_index = choose_distinct(own_keys[8], TOKENS, ADAPTER_EXPERTS, 2, 2048)
    routing_weight_pair = jnp.clip(jax.random.uniform(own_keys[9], (TOKENS, 2), jnp.float32, 0.2, 1.0), 0.2, 1.0)
    return dict(output_gradient=output_gradient, gate_preactivation=gate_preactivation, up_preactivation=up_preactivation, frozen_down_weight=frozen_down_weight, adapter_input_factor=adapter_input_factor, adapter_output_factor=adapter_output_factor, tenant_token_count=tenant_token_count, tenant_owner_index=tenant_owner_index, token_expert_index=token_expert_index, routing_weight_pair=routing_weight_pair)


adapter_scale = 2.0


def tables(tenant_token_count, tenant_owner_index, token_expert_index, routing_weight_pair):
    ends = jnp.cumsum(tenant_token_count).astype(jnp.int32)
    positions = jnp.arange(TOKENS, dtype=jnp.int32)
    token_tenant = jnp.sum((positions[:, None] >= ends[None, :]).astype(jnp.int32), axis=1).astype(jnp.int32)
    tenant_ids = jnp.arange(TENANT_COUNT, dtype=jnp.int32)
    tenant_hot = (token_tenant[:, None] == tenant_ids[None, :]).astype(jnp.float32)
    token_slot = jnp.sum(tenant_hot.astype(jnp.int32) * tenant_owner_index[None, :], axis=1).astype(jnp.int32)
    slot_hot = (token_slot[:, None] == tenant_ids[None, :]).astype(jnp.float32)
    expert_col = (jnp.arange(ADAPTER_EXPERTS * EXPERT_RANK, dtype=jnp.int32) // EXPERT_RANK)[None, :]
    mix = routing_weight_pair[:, 0:1] * (token_expert_index[:, 0:1] == expert_col).astype(jnp.float32)
    mix = mix + routing_weight_pair[:, 1:2] * (token_expert_index[:, 1:2] == expert_col).astype(jnp.float32)
    return tenant_hot, slot_hot, mix


def reference(output_gradient, gate_preactivation, up_preactivation, frozen_down_weight, adapter_input_factor, adapter_output_factor, tenant_token_count, tenant_owner_index, token_expert_index, routing_weight_pair):
    highest = lax.Precision.HIGHEST
    tenant_hot, slot_hot, mix = tables(tenant_token_count, tenant_owner_index, token_expert_index, routing_weight_pair)
    gate = gate_preactivation.astype(jnp.float32)
    up = up_preactivation.astype(jnp.float32)
    sig = jax.nn.sigmoid(gate)
    silu = gate * sig
    hidden_wide = silu * up
    input_factor_wide = adapter_input_factor.astype(jnp.float32)
    dense = jnp.dot(output_gradient, frozen_down_weight.T, preferred_element_type=jnp.float32)
    query_every_tenant = jnp.einsum('bl,xpl->bxp', output_gradient.astype(jnp.float32), adapter_output_factor.astype(jnp.float32), precision=highest)
    q_rows = jnp.sum(query_every_tenant * slot_hot[:, :, None], axis=1)
    p_rows = adapter_scale * q_rows * mix
    spread_wide = p_rows[:, None, :] * tenant_hot[:, :, None]
    grad_hidden = dense + jnp.einsum('tsc,sfc->tf', spread_wide, input_factor_wide, precision=highest)
    d_up = (grad_hidden * silu).astype(jnp.bfloat16)
    d_gate = (grad_hidden * up * sig * (1.0 + gate * (1.0 - sig))).astype(jnp.bfloat16)
    z_every = jnp.einsum('tf,sfc->tsc', hidden_wide, input_factor_wide, precision=highest)
    z_rows = jnp.sum(z_every * tenant_hot[:, :, None], axis=1)
    r_rows = adapter_scale * z_rows * mix
    spread_r = r_rows[:, None, :] * slot_hot[:, :, None]
    grad_b = jnp.einsum('tsc,td->scd', spread_r, output_gradient.astype(jnp.float32), precision=highest)
    grad_a = jnp.einsum('tf,tsc->sfc', hidden_wide, spread_wide, precision=highest)
    return d_gate, d_up, grad_a, grad_b
```

```python
import functools

import jax
import jax.numpy as jnp
from jax import lax
from jax.experimental import pallas as pl
from jax.experimental.pallas import tpu as pltpu
from jax.sharding import PartitionSpec as P

EXPERT_RANK = 16
ADAPTER_SCALE = 2.0
F32 = jnp.float32
BF16 = jnp.bfloat16
NT = (((1,), (1,)), ((), ()))
TN = (((0,), (0,)), ((), ()))


def split_bf16(x):
    high = x.astype(BF16)
    return high, (x - high.astype(F32)).astype(BF16)


def gather_kernel(
    n, counts, owners, og, gate, up, weight, a_in, b_out, mix,
    dense_out, hid_out, q_out, grad_b_out,
    og_all, w_v, gate_v, up_v, a_v, b_v, hid, prod,
    z_part, z_got, z_all, q_part, q_peer, q_half, q_got, q_all, r_rows,
    load_sem, ring_send, ring_recv, prod_send, prod_recv,
    z_send, z_recv, q_send, q_recv, core_send, core_recv, out_sem,
):
    me = lax.axis_index("dp")
    core = lax.axis_index("tensor")
    other = 1 - core
    half_n = n // 2
    block = og.shape[0]
    sub = block // 2
    tokens = block * n
    rows = tokens // 2
    part = rows // n
    hidden = weight.shape[0]
    tenants = a_in.shape[0]
    span = a_in.shape[2]
    tile = 256 if hidden % 256 == 0 else 128

    def at_ring(position):
        position = lax.rem(position + 2 * n, n)
        return jnp.where(position < half_n, 2 * position, 2 * (n - 1 - position) + 1)

    position = jnp.where(lax.rem(me, 2) == 0, me // 2, n - 1 - me // 2)
    right, left = at_ring(position + 1), at_ring(position - 1)

    loads = []

    def load(source, target):
        copy = pltpu.make_async_copy(source, target, load_sem.at[len(loads)])
        copy.start()
        loads.append(copy)
        return copy

    gate_load = load(gate, gate_v)
    up_load = load(up, up_v)
    a_load = load(a_in, a_v)
    og_load = load(og, og_all.at[pl.ds(0, block)])
    w_load = load(weight, w_v)
    b_load = load(b_out, b_v)

    barrier = pltpu.get_barrier_semaphore()
    for step in range(1, n):
        pl.semaphore_signal(
            barrier, inc=1, device_id={"dp": lax.rem(me + step, n)},
            device_id_type=pl.DeviceIdType.MESH,
        )
    pl.semaphore_signal(
        barrier, inc=1, device_id={"tensor": other}, device_id_type=pl.DeviceIdType.MESH
    )
    pl.semaphore_wait(barrier, n)

    def slot(way, distance):
        if distance == 0:
            return 0
        if distance == half_n:
            return n - 1
        return 1 + 2 * (distance - 1) + way

    def origin(k):
        if k == 0:
            return me
        if k == n - 1:
            return at_ring(position + half_n)
        distance = (k - 1) // 2 + 1
        return at_ring(position - distance) if (k - 1) % 2 == 0 else at_ring(position + distance)

    def hop(way, distance, piece):
        if distance == 1:
            source = og.at[pl.ds(piece * sub, sub)]
        else:
            source = og_all.at[pl.ds(slot(way, distance - 1) * block + piece * sub, sub)]
        return pltpu.make_async_remote_copy(
            src_ref=source,
            dst_ref=og_all.at[pl.ds(slot(way, distance) * block + piece * sub, sub)],
            send_sem=ring_send.at[way, distance - 1, piece],
            recv_sem=ring_recv.at[way, distance - 1, piece],
            device_id={"dp": right if way == 0 else left},
            device_id_type=pl.DeviceIdType.MESH,
        )

    def piece_of(way, order):
        return order if way == 0 else 1 - order

    hops = {}

    def start_hop(way, distance, order):
        piece = piece_of(way, order)
        hops[way, distance, order] = hop(way, distance, piece)
        hops[way, distance, order].start()

    for order in range(2):
        for way in range(2):
            start_hop(way, 1, order)

    def forward(distance, order):
        for way in range(2):
            hops[way, distance, order].wait_recv()
            if distance + 1 < half_n or (distance + 1 == half_n and order == 0):
                start_hop(way, distance + 1, order)

    gate_load.wait()
    up_load.wait()
    height = 16

    def hidden_step(i, carry):
        at = pl.ds(pl.multiple_of(i * height, height), height)
        low_at = pl.ds(pl.multiple_of(rows + i * height, height), height)
        g = gate_v[at, :].astype(F32)
        high, low = split_bf16(g * jax.nn.sigmoid(g) * up_v[at, :].astype(F32))
        hid[at, :] = high
        hid[low_at, :] = low
        return carry

    lax.fori_loop(0, rows // height, hidden_step, 0)

    to_core = {"tensor": other}
    mine = pl.ds(core * rows, rows)
    theirs = pl.ds(other * rows, rows)
    hid_copies = []
    for term in range(2):
        source = hid.at[pl.ds(term * rows, rows)]
        remote = pltpu.make_async_remote_copy(
            src_ref=source, dst_ref=hid_out.at[term, mine],
            send_sem=core_send.at[term], recv_sem=core_recv.at[term],
            device_id=to_core, device_id_type=pl.DeviceIdType.MESH,
        )
        local = pltpu.make_async_copy(source, hid_out.at[term, mine], out_sem.at[term])
        remote.start()
        local.start()
        hid_copies.append((remote, local))

    first = core * rows

    def z_work(lower, upper):
        def body(i, start):
            end = start + counts[i]
            both = jnp.dot(hid[...], a_v[i], preferred_element_type=F32)
            at = lax.broadcasted_iota(jnp.int32, (rows, span), 0) + first
            inside = jnp.logical_and(at >= start, at < end)
            z_part[...] += jnp.where(inside, both[:rows] + both[rows:], 0.0)
            return end

        start = jnp.int32(0)
        for i in range(lower):
            start = start + counts[i]
        lax.fori_loop(lower, upper, body, start)

    def scatter(source, got, send, recv):
        copies = []
        for step in range(1, n):
            to = lax.rem(me + step, n)
            copy = pltpu.make_async_remote_copy(
                src_ref=source.at[pl.ds(pl.multiple_of(to * part, part), part)],
                dst_ref=got.at[step],
                send_sem=send.at[0, step], recv_sem=recv.at[0, step],
                device_id={"dp": to}, device_id_type=pl.DeviceIdType.MESH,
            )
            copy.start()
            copies.append(copy)
        return copies

    def spread(source, got, full, copies, send, recv):
        total = source[pl.ds(pl.multiple_of(me * part, part), part), :]
        for step in range(1, n):
            copies[step - 1].wait_recv()
            total = total + got[step]
        at = pl.ds(pl.multiple_of(first + me * part, part), part)
        full[at, :] = total
        out = []
        for step in range(1, n):
            to = lax.rem(me + step, n)
            copy = pltpu.make_async_remote_copy(
                src_ref=full.at[at], dst_ref=full.at[at],
                send_sem=send.at[1, step], recv_sem=recv.at[1, step],
                device_id={"dp": to}, device_id_type=pl.DeviceIdType.MESH,
            )
            copy.start()
            out.append(copy)
        return out

    def landed(full, recv, send):
        for step in range(1, n):
            source = lax.rem(me + n - step, n)
            at = pl.ds(pl.multiple_of(first + source * part, part), part)
            pltpu.make_async_remote_copy(
                src_ref=full.at[at], dst_ref=full.at[at],
                send_sem=send.at[1, step], recv_sem=recv.at[1, step],
                device_id={"dp": source}, device_id_type=pl.DeviceIdType.MESH,
            ).wait_recv()

    def swap_landed(full, index):
        pltpu.make_async_remote_copy(
            src_ref=full.at[theirs], dst_ref=full.at[theirs],
            send_sem=core_send.at[index], recv_sem=core_recv.at[index],
            device_id=to_core, device_id_type=pl.DeviceIdType.MESH,
        ).wait_recv()

    def swap(full, index):
        copy = pltpu.make_async_remote_copy(
            src_ref=full.at[mine], dst_ref=full.at[mine],
            send_sem=core_send.at[index], recv_sem=core_recv.at[index],
            device_id=to_core, device_id_type=pl.DeviceIdType.MESH,
        )
        copy.start()
        return copy

    own_start, own_end, running = jnp.int32(0), jnp.int32(0), jnp.int32(0)
    for i in range(tenants):
        hit = (owners[i] == me).astype(jnp.int32)
        own_start = own_start + hit * running
        running = running + counts[i]
        own_end = own_end + hit * running

    def own_mask(start, length):
        at = lax.broadcasted_iota(jnp.int32, (length, span), 0) + start
        return jnp.logical_and(at >= own_start, at < own_end)

    def product_copy(k):
        j = origin(k)
        local = lax.rem(j, half_n)
        rows_at = pl.ds(pl.multiple_of(local * block, block), block)
        source = prod.at[pl.ds(k * block, block)]
        return (
            j // half_n,
            pltpu.make_async_remote_copy(
                src_ref=source, dst_ref=dense_out.at[1, rows_at],
                send_sem=prod_send.at[k], recv_sem=prod_recv.at[local],
                device_id=to_core, device_id_type=pl.DeviceIdType.MESH,
            ),
            pltpu.make_async_copy(source, dense_out.at[0, rows_at], out_sem.at[2 + local]),
        )

    def dense_work(k, width):
        at = pl.ds(k * block, width * block)
        query = lax.dot_general(og_all[at, :], b_v[...], NT, preferred_element_type=F32)
        for w in range(width):
            j = origin(k + w)
            q_part[pl.ds(pl.multiple_of(j * block, block), block), :] = jnp.where(
                own_mask(j * block, block), query[w * block:(w + 1) * block], 0.0
            )

        def body(t, carry):
            cols = pl.ds(pl.multiple_of(t * tile, tile), tile)
            prod[at, cols] = lax.dot_general(
                og_all[at, :], w_v[cols, :], NT, preferred_element_type=F32
            )
            return carry

        lax.fori_loop(0, hidden // tile, body, 0)
        for w in range(width):
            side, copy, keep = product_copy(k + w)

            @pl.when(side == core)
            def _():
                keep.start()

            @pl.when(side != core)
            def _():
                copy.start()

    z_part[...] = jnp.zeros_like(z_part)
    a_load.wait()
    forward(1, 0)
    z_work(0, tenants // 2)
    forward(1, 1)
    z_work(tenants // 2, tenants)
    z_copies = scatter(z_part, z_got, z_send, z_recv)
    og_load.wait()
    w_load.wait()
    b_load.wait()
    z_spread = None
    dense_done = 0
    for distance in range(2, half_n):
        forward(distance, 0)
        if distance == 2:
            dense_work(0, 1)
        dense_work(slot(0, distance - 1), 2)
        dense_done = distance - 1
        forward(distance, 1)
        if z_spread is None:
            z_spread = spread(z_part, z_got, z_all, z_copies, z_send, z_recv)
    if z_spread is None:
        dense_work(0, 1)
        z_spread = spread(z_part, z_got, z_all, z_copies, z_send, z_recv)
    for distance in range(dense_done + 1, half_n):
        dense_work(slot(0, distance), 2)
    landed(z_all, z_recv, z_send)
    z_swap = swap(z_all, 2)
    for way in range(2):
        hops[way, half_n, 0].wait_recv()
    at = pl.ds((n - 1) * block, block)
    dense_work(n - 1, 1)

    q_core = pltpu.make_async_remote_copy(
        src_ref=q_part.at[theirs], dst_ref=q_peer,
        send_sem=core_send.at[3], recv_sem=core_recv.at[3],
        device_id=to_core, device_id_type=pl.DeviceIdType.MESH,
    )
    q_core.start()
    swap_landed(z_all, 2)

    def r_work(k):
        j = origin(k)
        here = pl.ds(pl.multiple_of(j * block, block), block)
        r = jnp.where(own_mask(j * block, block), ADAPTER_SCALE * z_all[here, :] * mix[here, :], 0.0)
        high, low = split_bf16(r)
        r_rows[pl.ds(k * block, block), :] = jnp.concatenate([high, low], axis=1)

    for k in range(n):
        r_work(k)
    q_core.wait_recv()
    q_half[...] = q_part[mine, :] + q_peer[...]
    q_copies = scatter(q_half, q_got, q_send, q_recv)

    def grad_b_step(t, carry):
        cols = pl.ds(pl.multiple_of(t * 256, 256), 256)
        both = lax.dot_general(r_rows[...], og_all[:, cols], TN, preferred_element_type=F32)
        grad_b_out[:, cols] = both[:span] + both[span:]
        return carry

    width = og.shape[1] // 256
    lax.fori_loop(0, width, grad_b_step, 0)
    q_spread = spread(q_half, q_got, q_all, q_copies, q_send, q_recv)

    landed(q_all, q_recv, q_send)
    q_swap = swap(q_all, 4)
    for k in range(n):
        side, copy, keep = product_copy(k)

        @pl.when(side == core)
        def _():
            keep.wait()
            copy.wait_recv()

        @pl.when(side != core)
        def _():
            copy.wait_send()

    for copy in hops.values():
        copy.wait_send()
    for copy in z_copies + z_spread + q_copies + q_spread + [z_swap, q_core, q_swap]:
        copy.wait_send()
    for term, (remote, local) in enumerate(hid_copies):
        remote.wait_send()
        local.wait()
        pltpu.make_async_remote_copy(
            src_ref=hid.at[pl.ds(term * rows, rows)], dst_ref=hid_out.at[term, theirs],
            send_sem=core_send.at[term], recv_sem=core_recv.at[term],
            device_id=to_core, device_id_type=pl.DeviceIdType.MESH,
        ).wait_recv()
    swap_landed(q_all, 4)
    q_out[...] = q_all[...]


def tail_kernel(
    tenants_here, counts, side, gate, up, dense, hid, a_in, q_all, mix,
    d_gate, d_up, grad_a, p_rows, p_turned, total, acc,
):
    tokens, span = q_all.shape
    rows, tile = gate.shape
    tenants = a_in.shape[0]
    core = side[0]
    first = core * rows

    @pl.when(pl.program_id(0) == 0)
    def _():
        p = ADAPTER_SCALE * q_all[...] * mix[...]
        turned_high, turned_low = split_bf16(jnp.transpose(p))
        p_turned[:span, :] = turned_high
        p_turned[span:, :] = turned_low
        start = pl.multiple_of(first, rows)
        high, low = split_bf16(
            ADAPTER_SCALE * q_all[pl.ds(start, rows), :] * mix[pl.ds(start, rows), :]
        )
        p_rows[:, :span] = high
        p_rows[:, span:] = low

    total[...] = dense[0] + dense[1]
    starts = [jnp.int32(0)]
    for i in range(tenants):
        starts.append(starts[i] + counts[i])
    for i in range(tenants):
        lower, upper = starts[i], starts[i + 1]

        @pl.when(jnp.logical_and(lower < first + rows, upper > first))
        def _():
            at = lax.broadcasted_iota(jnp.int32, (rows, 2 * span), 0) + first
            inside = jnp.logical_and(at >= lower, at < upper)
            left = jnp.where(inside, p_rows[...].astype(F32), 0.0).astype(BF16)
            factor = a_in[i]
            total[...] += lax.dot_general(
                left, jnp.concatenate([factor, factor], axis=1), NT, preferred_element_type=F32
            )

    height = 16

    def step(i, carry):
        at = pl.ds(pl.multiple_of(i * height, height), height)
        g = gate[at, :].astype(F32)
        u = up[at, :].astype(F32)
        dh = total[at, :]
        sig = jax.nn.sigmoid(g)
        d_up[at, :] = (dh * (g * sig)).astype(BF16)
        d_gate[at, :] = (dh * u * sig * (1.0 + g * (1.0 - sig))).astype(BF16)
        return carry

    lax.fori_loop(0, rows // height, step, 0, unroll=4)

    piece = 256
    for i in range(tenants_here):
        tenant = core * tenants_here + i
        lower = jnp.int32(0)
        for k in range(tenants):
            lower = lower + jnp.where(k < tenant, counts[k], 0)
        upper = lower + counts[tenant]
        acc[...] = jnp.zeros_like(acc)
        for t in range(tokens // piece):
            base = t * piece

            @pl.when(jnp.logical_and(lower < base + piece, upper > base))
            def _():
                at = lax.broadcasted_iota(jnp.int32, (2 * span, piece), 1) + base
                inside = jnp.logical_and(at >= lower, at < upper)
                left = jnp.where(inside, p_turned[:, base:base + piece].astype(F32), 0.0)
                left = left.astype(BF16)
                both = jnp.dot(left, hid[0, base:base + piece, :], preferred_element_type=F32)
                low = jnp.dot(left[:span], hid[1, base:base + piece, :], preferred_element_type=F32)
                acc[...] += both[:span] + both[span:] + low

        grad_a[i] = jnp.transpose(acc[...])


def shards(
    n, output_gradient, gate_preactivation, up_preactivation, frozen_down_weight,
    adapter_input_factor, adapter_output_factor, tenant_token_count, tenant_owner_index,
    token_expert_index, routing_weight_pair,
):
    tokens = token_expert_index.shape[0]
    rows, hidden = gate_preactivation.shape
    tenants, _, span = adapter_input_factor.shape
    block, width = output_gradient.shape
    half_n = n // 2
    part = rows // n
    expert_col = lax.broadcasted_iota(jnp.int32, (1, span), 1) // EXPERT_RANK
    mix = routing_weight_pair[:, 0:1] * (token_expert_index[:, 0:1] == expert_col).astype(F32)
    mix = mix + routing_weight_pair[:, 1:2] * (token_expert_index[:, 1:2] == expert_col).astype(F32)

    any_spec = pl.BlockSpec(memory_space=pl.ANY)
    smem = pl.BlockSpec(memory_space=pltpu.SMEM)
    vmem = pl.BlockSpec(memory_space=pltpu.VMEM)
    dma = pltpu.SemaphoreType.DMA
    dense, hid, q_all, grad_b = pl.pallas_call(
        functools.partial(gather_kernel, n),
        out_shape=(
            jax.ShapeDtypeStruct((2, rows, hidden), F32),
            jax.ShapeDtypeStruct((2, tokens, hidden), BF16),
            jax.ShapeDtypeStruct((tokens, span), F32),
            jax.ShapeDtypeStruct((span, width), F32),
        ),
        in_specs=[smem, smem] + [any_spec] * 6 + [vmem],
        out_specs=(any_spec, any_spec, vmem, vmem),
        scratch_shapes=[
            pltpu.VMEM((tokens, width), BF16),
            pltpu.VMEM((hidden, width), BF16),
            pltpu.VMEM((rows, hidden), BF16),
            pltpu.VMEM((rows, hidden), BF16),
            pltpu.VMEM((tenants, hidden, span), BF16),
            pltpu.VMEM((span, width), BF16),
            pltpu.VMEM((2 * rows, hidden), BF16),
            pltpu.VMEM((tokens, hidden), F32),
            pltpu.VMEM((rows, span), F32),
            pltpu.VMEM((n, part, span), F32),
            pltpu.VMEM((tokens, span), F32),
            pltpu.VMEM((tokens, span), F32),
            pltpu.VMEM((rows, span), F32),
            pltpu.VMEM((rows, span), F32),
            pltpu.VMEM((n, part, span), F32),
            pltpu.VMEM((tokens, span), F32),
            pltpu.VMEM((tokens, 2 * span), BF16),
            dma((6,)),
            dma((2, half_n, 2)),
            dma((2, half_n, 2)),
            dma((n,)),
            dma((half_n,)),
            dma((2, n)),
            dma((2, n)),
            dma((2, n)),
            dma((2, n)),
            dma((5,)),
            dma((5,)),
            dma((2 + half_n,)),
        ],
        compiler_params=pltpu.CompilerParams(
            collective_id=0, has_side_effects=True, vmem_limit_bytes=60 * 1024 * 1024
        ),
        name="gather_products",
    )(
        tenant_token_count, tenant_owner_index, output_gradient, gate_preactivation,
        up_preactivation, frozen_down_weight, adapter_input_factor, adapter_output_factor[0], mix,
    )

    side = lax.axis_index("tensor").astype(jnp.int32)[None]
    tile = 256 if hidden % 256 == 0 else 128
    here = tenants // 2
    wide = pl.BlockSpec((rows, tile), lambda f: (0, f))
    d_gate, d_up, grad_a = pl.pallas_call(
        functools.partial(tail_kernel, here),
        grid=(hidden // tile,),
        out_shape=(
            jax.ShapeDtypeStruct((rows, hidden), BF16),
            jax.ShapeDtypeStruct((rows, hidden), BF16),
            jax.ShapeDtypeStruct((here, hidden, span), F32),
        ),
        in_specs=[
            smem, smem, wide, wide,
            pl.BlockSpec((2, rows, tile), lambda f: (0, 0, f)),
            pl.BlockSpec((2, tokens, tile), lambda f: (0, 0, f)),
            pl.BlockSpec((tenants, tile, span), lambda f: (0, f, 0)),
            pl.BlockSpec((tokens, span), lambda f: (0, 0)),
            pl.BlockSpec((tokens, span), lambda f: (0, 0)),
        ],
        out_specs=(wide, wide, pl.BlockSpec((here, tile, span), lambda f: (0, f, 0))),
        scratch_shapes=[
            pltpu.VMEM((rows, 2 * span), BF16),
            pltpu.VMEM((2 * span, tokens), BF16),
            pltpu.VMEM((rows, tile), F32),
            pltpu.VMEM((span, tile), F32),
        ],
        compiler_params=pltpu.CompilerParams(vmem_limit_bytes=48 * 1024 * 1024),
        name="tail",
    )(
        tenant_token_count, side, gate_preactivation, up_preactivation, dense, hid,
        adapter_input_factor, q_all, mix,
    )
    return d_gate, d_up, grad_a, grad_b[None]


def solution(mesh):
    in_specs = (
        P(("groups", "dp"), "tensor"),
        P(("groups", "tensor"), "dp"),
        P(("groups", "tensor"), "dp"),
        P("dp", "tensor"),
        P("groups", "dp", None),
        P(("groups", "dp"), None, "tensor"),
        P("groups"),
        P("groups"),
        P("groups", None),
        P("groups", None),
    )
    out_specs = (
        P(("groups", "tensor"), "dp"),
        P(("groups", "tensor"), "dp"),
        P(("groups", "tensor"), "dp", None),
        P(("groups", "dp"), None, "tensor"),
    )
    return jax.shard_map(
        functools.partial(shards, mesh.shape["dp"]),
        mesh=mesh, in_specs=in_specs, out_specs=out_specs, check_vma=False,
    )
```

```python
import functools

import jax
import jax.numpy as jnp
from jax import lax
from jax.experimental import pallas as pl
from jax.experimental.pallas import tpu as pltpu
from jax.sharding import PartitionSpec as P

EXPERT_RANK = 16
ADAPTER_SCALE = 2.0
F32 = jnp.float32
BF16 = jnp.bfloat16
NT = (((1,), (1,)), ((), ()))
TN = (((0,), (0,)), ((), ()))


def split_bf16(x):
    high = x.astype(BF16)
    return high, (x - high.astype(F32)).astype(BF16)


def gather_kernel(
    n, counts, owners, og, gate, up, weight, a_in, b_out, mix,
    dense_out, hid_out, q_out, grad_b_out,
    og_all, w_v, gate_v, up_v, a_v, b_v, hid, prod,
    z_part, z_got, z_all, q_part, q_peer, q_half, q_got, q_all, r_rows,
    load_sem, ring_send, ring_recv, prod_send, prod_recv,
    z_send, z_recv, q_send, q_recv, core_send, core_recv, out_sem,
):
    me = lax.axis_index("dp")
    core = lax.axis_index("tensor")
    other = 1 - core
    half_n = n // 2
    block = og.shape[0]
    sub = block // 2
    tokens = block * n
    rows = tokens // 2
    part = rows // n
    hidden = weight.shape[0]
    tenants = a_in.shape[0]
    span = a_in.shape[2]
    tile = 256 if hidden % 256 == 0 else 128

    def at_ring(position):
        position = lax.rem(position + 2 * n, n)
        return jnp.where(position < half_n, 2 * position, 2 * (n - 1 - position) + 1)

    position = jnp.where(lax.rem(me, 2) == 0, me // 2, n - 1 - me // 2)
    right, left = at_ring(position + 1), at_ring(position - 1)

    loads = []

    def load(source, target):
        copy = pltpu.make_async_copy(source, target, load_sem.at[len(loads)])
        copy.start()
        loads.append(copy)
        return copy

    gate_load = load(gate, gate_v)
    up_load = load(up, up_v)
    a_load = load(a_in, a_v)
    og_load = load(og, og_all.at[pl.ds(0, block)])
    w_load = load(weight, w_v)
    b_load = load(b_out, b_v)

    barrier = pltpu.get_barrier_semaphore()
    for step in range(1, n):
        pl.semaphore_signal(
            barrier, inc=1, device_id={"dp": lax.rem(me + step, n)},
            device_id_type=pl.DeviceIdType.MESH,
        )
    pl.semaphore_signal(
        barrier, inc=1, device_id={"tensor": other}, device_id_type=pl.DeviceIdType.MESH
    )
    pl.semaphore_wait(barrier, n)

    def slot(way, distance):
        if distance == 0:
            return 0
        if distance == half_n:
            return n - 1
        return 1 + 2 * (distance - 1) + way

    def origin(k):
        if k == 0:
            return me
        if k == n - 1:
            return at_ring(position + half_n)
        distance = (k - 1) // 2 + 1
        return at_ring(position - distance) if (k - 1) % 2 == 0 else at_ring(position + distance)

    def hop(way, distance, piece):
        if distance == 1:
            source = og.at[pl.ds(piece * sub, sub)]
        else:
            source = og_all.at[pl.ds(slot(way, distance - 1) * block + piece * sub, sub)]
        return pltpu.make_async_remote_copy(
            src_ref=source,
            dst_ref=og_all.at[pl.ds(slot(way, distance) * block + piece * sub, sub)],
            send_sem=ring_send.at[way, distance - 1, piece],
            recv_sem=ring_recv.at[way, distance - 1, piece],
            device_id={"dp": right if way == 0 else left},
            device_id_type=pl.DeviceIdType.MESH,
        )

    def piece_of(way, order):
        return order if way == 0 else 1 - order

    hops = {}

    def start_hop(way, distance, order):
        piece = piece_of(way, order)
        hops[way, distance, order] = hop(way, distance, piece)
        hops[way, distance, order].start()

    for order in range(2):
        for way in range(2):
            start_hop(way, 1, order)

    def forward(distance, order):
        for way in range(2):
            hops[way, distance, order].wait_recv()
            if distance + 1 < half_n or (distance + 1 == half_n and order == 0):
                start_hop(way, distance + 1, order)

    gate_load.wait()
    up_load.wait()
    height = 16

    def hidden_step(i, carry):
        at = pl.ds(pl.multiple_of(i * height, height), height)
        low_at = pl.ds(pl.multiple_of(rows + i * height, height), height)
        g = gate_v[at, :].astype(F32)
        high, low = split_bf16(g * jax.nn.sigmoid(g) * up_v[at, :].astype(F32))
        hid[at, :] = high
        hid[low_at, :] = low
        return carry

    lax.fori_loop(0, rows // height, hidden_step, 0, unroll=2)

    to_core = {"tensor": other}
    mine = pl.ds(core * rows, rows)
    theirs = pl.ds(other * rows, rows)
    hid_copies = []
    for term in range(2):
        source = hid.at[pl.ds(term * rows, rows)]
        remote = pltpu.make_async_remote_copy(
            src_ref=source, dst_ref=hid_out.at[term, mine],
            send_sem=core_send.at[term], recv_sem=core_recv.at[term],
            device_id=to_core, device_id_type=pl.DeviceIdType.MESH,
        )
        local = pltpu.make_async_copy(source, hid_out.at[term, mine], out_sem.at[term])
        remote.start()
        local.start()
        hid_copies.append((remote, local))

    first = core * rows

    def z_work(lower, upper):
        def body(i, start):
            end = start + counts[i]
            both = jnp.dot(hid[...], a_v[i], preferred_element_type=F32)
            at = lax.broadcasted_iota(jnp.int32, (rows, span), 0) + first
            inside = jnp.logical_and(at >= start, at < end)
            z_part[...] += jnp.where(inside, both[:rows] + both[rows:], 0.0)
            return end

        start = jnp.int32(0)
        for i in range(lower):
            start = start + counts[i]
        lax.fori_loop(lower, upper, body, start)

    def scatter(source, got, send, recv):
        copies = []
        for step in range(1, n):
            to = lax.rem(me + step, n)
            copy = pltpu.make_async_remote_copy(
                src_ref=source.at[pl.ds(pl.multiple_of(to * part, part), part)],
                dst_ref=got.at[step],
                send_sem=send.at[0, step], recv_sem=recv.at[0, step],
                device_id={"dp": to}, device_id_type=pl.DeviceIdType.MESH,
            )
            copy.start()
            copies.append(copy)
        return copies

    def spread(source, got, full, copies, send, recv):
        total = source[pl.ds(pl.multiple_of(me * part, part), part), :]
        for step in range(1, n):
            copies[step - 1].wait_recv()
            total = total + got[step]
        at = pl.ds(pl.multiple_of(first + me * part, part), part)
        full[at, :] = total
        out = []
        for step in range(1, n):
            to = lax.rem(me + step, n)
            copy = pltpu.make_async_remote_copy(
                src_ref=full.at[at], dst_ref=full.at[at],
                send_sem=send.at[1, step], recv_sem=recv.at[1, step],
                device_id={"dp": to}, device_id_type=pl.DeviceIdType.MESH,
            )
            copy.start()
            out.append(copy)
        return out

    def landed(full, recv, send):
        for step in range(1, n):
            source = lax.rem(me + n - step, n)
            at = pl.ds(pl.multiple_of(first + source * part, part), part)
            pltpu.make_async_remote_copy(
                src_ref=full.at[at], dst_ref=full.at[at],
                send_sem=send.at[1, step], recv_sem=recv.at[1, step],
                device_id={"dp": source}, device_id_type=pl.DeviceIdType.MESH,
            ).wait_recv()

    def swap_landed(full, index):
        pltpu.make_async_remote_copy(
            src_ref=full.at[theirs], dst_ref=full.at[theirs],
            send_sem=core_send.at[index], recv_sem=core_recv.at[index],
            device_id=to_core, device_id_type=pl.DeviceIdType.MESH,
        ).wait_recv()

    def swap(full, index):
        copy = pltpu.make_async_remote_copy(
            src_ref=full.at[mine], dst_ref=full.at[mine],
            send_sem=core_send.at[index], recv_sem=core_recv.at[index],
            device_id=to_core, device_id_type=pl.DeviceIdType.MESH,
        )
        copy.start()
        return copy

    own_start, own_end, running = jnp.int32(0), jnp.int32(0), jnp.int32(0)
    for i in range(tenants):
        hit = (owners[i] == me).astype(jnp.int32)
        own_start = own_start + hit * running
        running = running + counts[i]
        own_end = own_end + hit * running

    def own_mask(start, length):
        at = lax.broadcasted_iota(jnp.int32, (length, span), 0) + start
        return jnp.logical_and(at >= own_start, at < own_end)

    def product_copy(k):
        j = origin(k)
        local = lax.rem(j, half_n)
        rows_at = pl.ds(pl.multiple_of(local * block, block), block)
        source = prod.at[pl.ds(k * block, block)]
        return (
            j // half_n,
            pltpu.make_async_remote_copy(
                src_ref=source, dst_ref=dense_out.at[1, rows_at],
                send_sem=prod_send.at[k], recv_sem=prod_recv.at[local],
                device_id=to_core, device_id_type=pl.DeviceIdType.MESH,
            ),
            pltpu.make_async_copy(source, dense_out.at[0, rows_at], out_sem.at[2 + local]),
        )

    def query_work(k, width):
        at = pl.ds(k * block, width * block)
        query = lax.dot_general(og_all[at, :], b_v[...], NT, preferred_element_type=F32)
        for w in range(width):
            j = origin(k + w)
            q_part[pl.ds(pl.multiple_of(j * block, block), block), :] = jnp.where(
                own_mask(j * block, block), query[w * block:(w + 1) * block], 0.0
            )

    def dense_work(k, width):
        if k < n - 1:
            query_work(k, width)
        at = pl.ds(k * block, width * block)

        def body(t, carry):
            cols = pl.ds(pl.multiple_of(t * tile, tile), tile)
            prod[at, cols] = lax.dot_general(
                og_all[at, :], w_v[cols, :], NT, preferred_element_type=F32
            )
            return carry

        lax.fori_loop(0, hidden // tile, body, 0)
        for w in range(width):
            side, copy, keep = product_copy(k + w)

            @pl.when(side == core)
            def _():
                keep.start()

            @pl.when(side != core)
            def _():
                copy.start()

    z_part[...] = jnp.zeros_like(z_part)
    a_load.wait()
    forward(1, 0)
    z_work(0, tenants // 2)
    forward(1, 1)
    z_work(tenants // 2, tenants)
    z_copies = scatter(z_part, z_got, z_send, z_recv)
    og_load.wait()
    w_load.wait()
    b_load.wait()
    z_spread = None
    dense_done = 0
    for distance in range(2, half_n):
        forward(distance, 0)
        if distance == 2:
            dense_work(0, 1)
        dense_work(slot(0, distance - 1), 2)
        dense_done = distance - 1
        forward(distance, 1)
        if z_spread is None:
            z_spread = spread(z_part, z_got, z_all, z_copies, z_send, z_recv)
    if z_spread is None:
        dense_work(0, 1)
        z_spread = spread(z_part, z_got, z_all, z_copies, z_send, z_recv)
    for distance in range(dense_done + 1, half_n):
        dense_work(slot(0, distance), 2)
    landed(z_all, z_recv, z_send)
    z_swap = swap(z_all, 2)
    for way in range(2):
        hops[way, half_n, 0].wait_recv()
    query_work(n - 1, 1)

    q_core = pltpu.make_async_remote_copy(
        src_ref=q_part.at[theirs], dst_ref=q_peer,
        send_sem=core_send.at[3], recv_sem=core_recv.at[3],
        device_id=to_core, device_id_type=pl.DeviceIdType.MESH,
    )
    q_core.start()
    swap_landed(z_all, 2)

    def r_work(k):
        j = origin(k)
        here = pl.ds(pl.multiple_of(j * block, block), block)
        r = jnp.where(own_mask(j * block, block), ADAPTER_SCALE * z_all[here, :] * mix[here, :], 0.0)
        high, low = split_bf16(r)
        r_rows[pl.ds(k * block, block), :] = jnp.concatenate([high, low], axis=1)

    for k in range(n):
        r_work(k)
    q_core.wait_recv()
    q_half[...] = q_part[mine, :] + q_peer[...]
    q_copies = scatter(q_half, q_got, q_send, q_recv)
    dense_work(n - 1, 1)

    def grad_b_step(t, carry):
        cols = pl.ds(pl.multiple_of(t * 256, 256), 256)
        both = lax.dot_general(r_rows[...], og_all[:, cols], TN, preferred_element_type=F32)
        grad_b_out[:, cols] = both[:span] + both[span:]
        return carry

    q_spread = spread(q_half, q_got, q_all, q_copies, q_send, q_recv)
    lax.fori_loop(0, og.shape[1] // 256, grad_b_step, 0)
    landed(q_all, q_recv, q_send)
    q_swap = swap(q_all, 4)
    for k in range(n):
        side, copy, keep = product_copy(k)

        @pl.when(side == core)
        def _():
            keep.wait()
            copy.wait_recv()

        @pl.when(side != core)
        def _():
            copy.wait_send()

    for copy in hops.values():
        copy.wait_send()
    for copy in z_copies + z_spread + q_copies + q_spread + [z_swap, q_core, q_swap]:
        copy.wait_send()
    for term, (remote, local) in enumerate(hid_copies):
        remote.wait_send()
        local.wait()
        pltpu.make_async_remote_copy(
            src_ref=hid.at[pl.ds(term * rows, rows)], dst_ref=hid_out.at[term, theirs],
            send_sem=core_send.at[term], recv_sem=core_recv.at[term],
            device_id=to_core, device_id_type=pl.DeviceIdType.MESH,
        ).wait_recv()
    swap_landed(q_all, 4)
    q_out[...] = q_all[...]


def tail_kernel(
    tenants_here, counts, side, gate, up, dense, hid, a_in, q_all, mix,
    d_gate, d_up, grad_a, p_rows, p_turned, total, acc,
):
    tokens, span = q_all.shape
    rows, tile = gate.shape
    tenants = a_in.shape[0]
    core = side[0]
    first = core * rows

    starts = [jnp.int32(0)]
    for i in range(tenants):
        starts.append(starts[i] + counts[i])
    bounds = []
    for i in range(tenants_here):
        upper_half = core == 1
        bounds.append((
            jnp.where(upper_half, starts[tenants_here + i], starts[i]),
            jnp.where(upper_half, starts[tenants_here + i + 1], starts[i + 1]),
        ))

    @pl.when(pl.program_id(0) == 0)
    def _():
        p = ADAPTER_SCALE * q_all[...] * mix[...]
        turned = jnp.transpose(p)
        at = lax.broadcasted_iota(jnp.int32, (span, tokens), 1)
        for i in range(tenants_here):
            inside = jnp.logical_and(at >= bounds[i][0], at < bounds[i][1])
            high, low = split_bf16(jnp.where(inside, turned, 0.0))
            p_turned[i, :span, :] = high
            p_turned[i, span:, :] = low
        start = pl.multiple_of(first, rows)
        own = ADAPTER_SCALE * q_all[pl.ds(start, rows), :] * mix[pl.ds(start, rows), :]
        at = lax.broadcasted_iota(jnp.int32, (rows, span), 0) + first
        for i in range(tenants):
            inside = jnp.logical_and(at >= starts[i], at < starts[i + 1])
            high, low = split_bf16(jnp.where(inside, own, 0.0))
            p_rows[:, 2 * i * span:(2 * i + 1) * span] = high
            p_rows[:, (2 * i + 1) * span:(2 * i + 2) * span] = low

    factors = jnp.concatenate([a_in[i // 2] for i in range(2 * tenants)], axis=1)
    total[...] = lax.dot_general(p_rows[...], factors, NT, preferred_element_type=F32)

    height = 32

    def step(i, carry):
        at = pl.ds(pl.multiple_of(i * height, height), height)
        g = gate[at, :].astype(F32)
        u = up[at, :].astype(F32)
        dh = total[at, :] + (dense[0, at, :] + dense[1, at, :])
        sig = jax.nn.sigmoid(g)
        d_up[at, :] = (dh * (g * sig)).astype(BF16)
        d_gate[at, :] = (dh * u * sig * (1.0 + g * (1.0 - sig))).astype(BF16)
        return carry

    lax.fori_loop(0, rows // height, step, 0, unroll=4)

    piece = 512
    for i in range(tenants_here):
        lower, upper = bounds[i]
        acc[...] = jnp.zeros_like(acc)
        for t in range(tokens // piece):
            base = t * piece

            @pl.when(jnp.logical_and(lower < base + piece, upper > base))
            def _():
                left = p_turned[i, :, base:base + piece]
                both = jnp.dot(left, hid[0, base:base + piece, :], preferred_element_type=F32)
                low = jnp.dot(left[:span], hid[1, base:base + piece, :], preferred_element_type=F32)
                acc[...] += both[:span] + both[span:] + low

        grad_a[i] = jnp.transpose(acc[...])


def shards(
    n, output_gradient, gate_preactivation, up_preactivation, frozen_down_weight,
    adapter_input_factor, adapter_output_factor, tenant_token_count, tenant_owner_index,
    token_expert_index, routing_weight_pair,
):
    tokens = token_expert_index.shape[0]
    rows, hidden = gate_preactivation.shape
    tenants, _, span = adapter_input_factor.shape
    block, width = output_gradient.shape
    half_n = n // 2
    part = rows // n
    expert_col = lax.broadcasted_iota(jnp.int32, (1, span), 1) // EXPERT_RANK
    mix = routing_weight_pair[:, 0:1] * (token_expert_index[:, 0:1] == expert_col).astype(F32)
    mix = mix + routing_weight_pair[:, 1:2] * (token_expert_index[:, 1:2] == expert_col).astype(F32)

    any_spec = pl.BlockSpec(memory_space=pl.ANY)
    smem = pl.BlockSpec(memory_space=pltpu.SMEM)
    vmem = pl.BlockSpec(memory_space=pltpu.VMEM)
    dma = pltpu.SemaphoreType.DMA
    dense, hid, q_all, grad_b = pl.pallas_call(
        functools.partial(gather_kernel, n),
        out_shape=(
            jax.ShapeDtypeStruct((2, rows, hidden), F32),
            jax.ShapeDtypeStruct((2, tokens, hidden), BF16),
            jax.ShapeDtypeStruct((tokens, span), F32),
            jax.ShapeDtypeStruct((span, width), F32),
        ),
        in_specs=[smem, smem] + [any_spec] * 6 + [vmem],
        out_specs=(any_spec, any_spec, vmem, vmem),
        scratch_shapes=[
            pltpu.VMEM((tokens, width), BF16),
            pltpu.VMEM((hidden, width), BF16),
            pltpu.VMEM((rows, hidden), BF16),
            pltpu.VMEM((rows, hidden), BF16),
            pltpu.VMEM((tenants, hidden, span), BF16),
            pltpu.VMEM((span, width), BF16),
            pltpu.VMEM((2 * rows, hidden), BF16),
            pltpu.VMEM((tokens, hidden), F32),
            pltpu.VMEM((rows, span), F32),
            pltpu.VMEM((n, part, span), F32),
            pltpu.VMEM((tokens, span), F32),
            pltpu.VMEM((tokens, span), F32),
            pltpu.VMEM((rows, span), F32),
            pltpu.VMEM((rows, span), F32),
            pltpu.VMEM((n, part, span), F32),
            pltpu.VMEM((tokens, span), F32),
            pltpu.VMEM((tokens, 2 * span), BF16),
            dma((6,)),
            dma((2, half_n, 2)),
            dma((2, half_n, 2)),
            dma((n,)),
            dma((half_n,)),
            dma((2, n)),
            dma((2, n)),
            dma((2, n)),
            dma((2, n)),
            dma((5,)),
            dma((5,)),
            dma((2 + half_n,)),
        ],
        compiler_params=pltpu.CompilerParams(
            collective_id=0, has_side_effects=True, vmem_limit_bytes=60 * 1024 * 1024
        ),
        name="gather_products",
    )(
        tenant_token_count, tenant_owner_index, output_gradient, gate_preactivation,
        up_preactivation, frozen_down_weight, adapter_input_factor, adapter_output_factor[0], mix,
    )

    side = lax.axis_index("tensor").astype(jnp.int32)[None]
    tile = 256 if hidden % 256 == 0 else 128
    here = tenants // 2
    wide = pl.BlockSpec((rows, tile), lambda f: (0, f))
    d_gate, d_up, grad_a = pl.pallas_call(
        functools.partial(tail_kernel, here),
        grid=(hidden // tile,),
        out_shape=(
            jax.ShapeDtypeStruct((rows, hidden), BF16),
            jax.ShapeDtypeStruct((rows, hidden), BF16),
            jax.ShapeDtypeStruct((here, hidden, span), F32),
        ),
        in_specs=[
            smem, smem, wide, wide,
            pl.BlockSpec((2, rows, tile), lambda f: (0, 0, f)),
            pl.BlockSpec((2, tokens, tile), lambda f: (0, 0, f)),
            pl.BlockSpec((tenants, tile, span), lambda f: (0, f, 0)),
            pl.BlockSpec((tokens, span), lambda f: (0, 0)),
            pl.BlockSpec((tokens, span), lambda f: (0, 0)),
        ],
        out_specs=(wide, wide, pl.BlockSpec((here, tile, span), lambda f: (0, f, 0))),
        scratch_shapes=[
            pltpu.VMEM((rows, 2 * tenants * span), BF16),
            pltpu.VMEM((here, 2 * span, tokens), BF16),
            pltpu.VMEM((rows, tile), F32),
            pltpu.VMEM((span, tile), F32),
        ],
        compiler_params=pltpu.CompilerParams(vmem_limit_bytes=48 * 1024 * 1024),
        name="tail",
    )(
        tenant_token_count, side, gate_preactivation, up_preactivation, dense, hid,
        adapter_input_factor, q_all, mix,
    )
    return d_gate, d_up, grad_a, grad_b[None]


def solution(mesh):
    in_specs = (
        P(("groups", "dp"), "tensor"),
        P(("groups", "tensor"), "dp"),
        P(("groups", "tensor"), "dp"),
        P("dp", "tensor"),
        P("groups", "dp", None),
        P(("groups", "dp"), None, "tensor"),
        P("groups"),
        P("groups"),
        P("groups", None),
        P("groups", None),
    )
    out_specs = (
        P(("groups", "tensor"), "dp"),
        P(("groups", "tensor"), "dp"),
        P(("groups", "tensor"), "dp", None),
        P(("groups", "dp"), None, "tensor"),
    )
    return jax.shard_map(
        functools.partial(shards, mesh.shape["dp"]),
        mesh=mesh, in_specs=in_specs, out_specs=out_specs, check_vma=False,
    )
```
